512 devices in a mesh: arow: 16 (over z), acol: 16 (over y_lo, x, core), occ: 2 (over y_hi).
Axes of the slice: x: 4, y: 4 (y_hi: 2, y_lo: 2; y = y_hi * 2 + y_lo), z: 16, core: 2. Of those that a mesh axis runs over, the one named last changes fastest.
Arguments:
- factors: bfloat16 [16, 4096, 3072], P('occ', ('arow', 'acol')), may hold values from -0.5 to 0.5
- occ_energies: float32 [300], replicated, may hold values from -1.2 to -0.3
- virt_energies: float32 [3072], replicated, may hold values from 0.1 to 4
- freq_grid: float32 [32], replicated, may hold values from 0.05 to 20
- occ_index: int32 [16], P('occ'), may hold values from 0 to 299
- virt_index: int32 [3072], replicated, may hold values from 0 to 3071
- freq_index: int32 [1], replicated, may hold values from 0 to 31
Outputs:
- response: float32 [4096, 4096], P('arow', 'acol')
The draws below stay inside these ranges and needn't reach their ends.
All inputs are finite; a program needn't handle non-finite values.
Results may differ from the reference program's by a relative error of at most 0.00085.
Values may be sent and summed in bfloat16 or wider, within the bound.
No kernel may reach another device: no remote copies, remote signals or barrier semaphores. Data moves between devices by JAX's collectives and lax.ppermute only.
A program may use at most 64 MiB of HBM per device.

```python
import math
import jax
import jax.numpy as jnp
from jax import lax

NAUX = 4096
NV = 3072
NOCC_ALL = 300
NFREQ = 32
WINDOW = 16


def set_ends(result, own_key, least, high):
    extent = result.shape
    index_at = [jax.random.randint(jax.random.fold_in(own_key, axis), (), 0, extent[axis]) for axis in range(len(extent))]
    result = result.at[tuple(index_at)].set(least)
    longest = extent.index(max(extent))
    index_at[longest] = (index_at[longest] + 1) % extent[longest]
    return result.at[tuple(index_at)].set(high)


def with_spikes(entries, rng, source, target, parts, factor):
    owner, partner = [(jnp.arange(entries.shape[axis_at]) // (entries.shape[axis_at] // parts)).reshape([-1 if axis == axis_at else 1 for axis in range(entries.ndim)]) for axis_at in (source, target)]
    chosen = jax.random.permutation(rng, parts)[partner]
    strong = (owner == chosen) | (owner == (partner + parts // 2) % parts)
    return jnp.where(strong, factor * entries, entries)


def shard_levels(stream_key, extent, pieces, smallest, top_value):
    def one(position, parts):
        steps = jax.random.uniform(jax.random.fold_in(jax.random.fold_in(stream_key, 6), position), (parts,), jnp.float32, smallest / len(pieces), top_value / len(pieces))
        return jnp.repeat(jnp.exp(steps), extent[position] // parts).reshape((-1,) + (1,) * (len(extent) - position - 1))

    level = one(*pieces[0])
    for cut in pieces[1:]:
        level = level * one(*cut)
    return level


def noise_with(stream_key, shape, spread, reach, shards, heavy, kind=jnp.bfloat16):
    entries = spread * jax.random.normal(stream_key, shape, jnp.float32)
    if shards:
        entries = entries * shard_levels(stream_key, shape, shards, -0.22, 0.18)
    return jnp.clip(with_spikes(entries, jax.random.fold_in(stream_key, 3), *heavy), -reach, reach).astype(kind)


def setup_inputs(seed: int = 0) -> dict:
    key_list = jax.random.split(jax.random.key(seed), 8)
    return {
        "factors": noise_with(key_list[0], (WINDOW, NAUX, NV), 0.02, 0.5, ((0, 2), (1, 256)), (2, 1, 256, 6.0)),
        "occ_energies": jnp.clip(jax.random.uniform(key_list[1], (NOCC_ALL,), jnp.float32, -1.2, -0.3), -1.2, -0.3),
        "virt_energies": jnp.clip(jax.random.uniform(key_list[2], (NV,), jnp.float32, 0.1, 4.0), 0.1, 4.0),
        "freq_grid": jnp.clip(jnp.exp(jax.random.uniform(key_list[3], (NFREQ,), jnp.float32, math.log(0.05), math.log(20.0))), 0.05, 20.0),
        "occ_index": set_ends(jax.random.randint(key_list[4], (WINDOW,), 0, NOCC_ALL), jax.random.fold_in(key_list[4], 1), 0, NOCC_ALL - 1).astype(jnp.int32),
        "virt_index": set_ends(jax.random.randint(key_list[5], (NV,), 0, NV), jax.random.fold_in(key_list[5], 1), 0, NV - 1).astype(jnp.int32),
        "freq_index": jax.random.randint(key_list[6], (1,), 0, NFREQ).astype(jnp.int32),
    }


def reference(factors, occ_energies, virt_energies, freq_grid, occ_index, virt_index, freq_index):
    frequency = freq_grid[freq_index[0]]
    excitation = virt_energies[virt_index][None, :] - occ_energies[occ_index][:, None]
    weight = -4.0 * excitation / (excitation * excitation + frequency * frequency)

    def accumulate(total, orbital):
        matrix = lax.dynamic_index_in_dim(factors, orbital, 0, keepdims=False).astype(jnp.float32)
        row_weight = lax.dynamic_index_in_dim(weight, orbital, 0, keepdims=False)
        scaled = (matrix * row_weight[None, :]).astype(jnp.bfloat16).astype(jnp.float32)
        product = jnp.dot(scaled, matrix.T, precision=lax.Precision.HIGHEST, preferred_element_type=jnp.float32)
        return total + product, None

    start = jnp.zeros((NAUX, NAUX), jnp.float32)
    total, unused = lax.scan(accumulate, start, jnp.arange(WINDOW, dtype=jnp.int32))
    return total
```

```python
import functools

import jax
import jax.numpy as jnp
from jax import lax
from jax.experimental import pallas as pl
from jax.experimental.pallas import tpu as pltpu
from jax.sharding import Mesh
from jax.sharding import PartitionSpec as P

AXES = ("z", "ylo", "x", "core", "yhi")
Y_RING = ("ylo", "core", "yhi")
VMEM_LIMIT = 56 * 1024 * 1024


def lookup(table, indices):
    positions = jnp.arange(table.shape[0], dtype=jnp.int32)
    hits = indices[:, None] == positions[None, :]
    return jnp.sum(jnp.where(hits, table[None, :], jnp.float32(0.0)), axis=1)


def pack_kernel(src, dst):
    half = src.shape[2] // 2
    dst[0] = src[0, :, :half]
    dst[1] = src[0, :, half:]


def pack(factors):
    orbitals, rows, virt = factors.shape
    return pl.pallas_call(
        pack_kernel,
        grid=(orbitals,),
        in_specs=[pl.BlockSpec((1, rows, virt), lambda w: (w, 0, 0))],
        out_specs=pl.BlockSpec((2, rows, virt // 2), lambda w: (w, 0, 0)),
        out_shape=jax.ShapeDtypeStruct((2 * orbitals, rows, virt // 2), factors.dtype),
    )(factors)


def product_kernel(place, weight, p0, p1, p2, p3, q00, q01, q10, q11, out, left, right):
    step = pl.program_id(0)
    x, ylo, yhi = place[0], place[1], place[2]
    rows, depth = p0.shape
    planes = rows // 16

    @pl.when(step == 0)
    def _():
        for shift, block in enumerate((p0, p1, p2, p3)):
            at = lax.rem(x + 4 - shift, 4)

            def scale(r, carry, block=block, at=at):
                chunk = block[pl.ds(pl.multiple_of(r * 16, 16), 16), :]
                left[r, at] = (chunk.astype(jnp.float32) * weight[...]).astype(jnp.bfloat16)
                return carry

            lax.fori_loop(0, planes, scale, 0)
        for bits, block in (((0, 0), q00), ((0, 1), q01), ((1, 0), q10), ((1, 1), q11)):
            at = (ylo ^ bits[1]) * 2 + (yhi ^ bits[0])

            def move(r, carry, block=block, at=at):
                right[r, at] = block[pl.ds(pl.multiple_of(r * 16, 16), 16), :]
                return carry

            lax.fori_loop(0, planes, move, 0)

    columns = right[pl.ds(step * 4, 4)].reshape(256, depth)
    low = lax.broadcasted_iota(jnp.int32, (32, 128), 1) < 64

    def tile(m, carry):
        block = left[pl.ds(m * 4, 4)].reshape(256, depth)
        total = lax.dot_general(
            block, columns, (((1,), (1,)), ((), ())), preferred_element_type=jnp.float32
        )
        for r in range(4):
            for pair in range(2):
                lanes = slice(pair * 128, pair * 128 + 128)
                first = total[r * 64 : r * 64 + 32, lanes]
                second = total[r * 64 + 32 : r * 64 + 64, lanes]
                out[m * 4 + r, 2 * pair] = jnp.where(low, first, pltpu.roll(second, 64, 1))
                out[m * 4 + r, 2 * pair + 1] = jnp.where(low, pltpu.roll(first, 64, 1), second)
        return carry

    lax.fori_loop(0, 4, tile, 0)


def product(place, weight, p_blocks, q_blocks):
    rows, depth = p_blocks[0].shape
    whole = pl.BlockSpec(memory_space=pltpu.VMEM)
    return pl.pallas_call(
        product_kernel,
        grid=(4,),
        in_specs=[pl.BlockSpec(memory_space=pltpu.SMEM)] + [whole] * 9,
        out_specs=pl.BlockSpec((16, 4, 32, 128), lambda n: (0, n, 0, 0)),
        out_shape=jax.ShapeDtypeStruct((16, 16, 32, 128), jnp.float32),
        scratch_shapes=[pltpu.VMEM((16, 4, 16, depth), jnp.bfloat16)] * 2,
        compiler_params=pltpu.CompilerParams(vmem_limit_bytes=VMEM_LIMIT),
        cost_estimate=pl.CostEstimate(
            flops=2 * 1024 * 1024 * depth, bytes_accessed=10 * 1024 * 1024, transcendentals=0
        ),
    )(place, weight, *p_blocks, *q_blocks)


def collect_kernel(parts, out):
    lane = lax.broadcasted_iota(jnp.int32, (32, 128), 1) // 32
    for ylo in range(2):
        sums = [parts[ylo * 8 + x * 2] + parts[ylo * 8 + x * 2 + 1] for x in range(4)]
        for high in range(2):
            for column in range(2):
                start = high * 64 + column * 32
                total = jnp.zeros((32, 128), jnp.float32)
                for x in range(4):
                    shift = (x * 32 - start) % 128
                    moved = pltpu.roll(sums[x], shift, 1) if shift else sums[x]
                    total = jnp.where(lane == x, moved, total)
                lanes = slice(column * 128, column * 128 + 128)
                out[ylo * 4 + high * 2, :, lanes] = total[:16]
                out[ylo * 4 + high * 2 + 1, :, lanes] = total[16:]


def collect(parts):
    return pl.pallas_call(
        collect_kernel, out_shape=jax.ShapeDtypeStruct((8, 16, 256), jnp.float32)
    )(parts)


def merge_kernel(place, mine, other, out):
    yhi = place[2]
    for group in range(8):
        a, b = mine[group], other[group]
        out[pl.ds(group * 32, 16), :] = jnp.where(yhi == 0, a, b)
        out[pl.ds(group * 32 + 16, 16), :] = jnp.where(yhi == 0, b, a)


def merge(place, mine, other):
    whole = pl.BlockSpec(memory_space=pltpu.VMEM)
    return pl.pallas_call(
        merge_kernel,
        in_specs=[pl.BlockSpec(memory_space=pltpu.SMEM), whole, whole],
        out_specs=whole,
        out_shape=jax.ShapeDtypeStruct((256, 256), jnp.float32),
    )(place, mine, other)


def ring_permutation(s, t):
    index = lambda ylo, core, yhi: (ylo * 2 + core) * 2 + yhi
    return [
        (index(ylo, core, yhi), index(ylo ^ t, yhi, core ^ s))
        for ylo in range(2)
        for core in range(2)
        for yhi in range(2)
    ]


def body(factors, occ_energies, virt_energies, freq_grid, occ_index, virt_index, freq_index):
    z, ylo, x, core, yhi = (lax.axis_index(a) for a in AXES)
    place = jnp.stack([x, ylo, yhi]).astype(jnp.int32)
    own_index = lax.ppermute(occ_index, Y_RING, ring_permutation(0, 0))
    planes = lax.all_to_all(pack(factors), "z", split_axis=0, concat_axis=0, tiled=True)
    depth = planes.shape[2]
    rows = planes.reshape(-1, depth)

    own_virtual = lax.dynamic_slice_in_dim(virt_index, (z % 2) * depth, depth)
    own_occupied = lax.dynamic_slice_in_dim(own_index, z // 2, 1)
    excitation = lookup(virt_energies, own_virtual) - lookup(occ_energies, own_occupied)
    frequency = lookup(freq_grid, freq_index)[0]
    weight = -4.0 * excitation / (excitation * excitation + frequency * frequency)

    q_blocks = [
        lax.ppermute(rows, Y_RING, ring_permutation(s, t)) for s, t in ((0, 0), (0, 1), (1, 0), (1, 1))
    ]
    own = q_blocks[0]
    p_blocks = [own] + [
        lax.ppermute(own, "x", [(i, (i + shift) % 4) for i in range(4)]) for shift in (1, 2, 3)
    ]
    partial = product(place, weight[None, :], p_blocks, q_blocks)
    plane = lax.psum_scatter(partial, "z", scatter_dimension=0, tiled=True)[0]
    parts = lax.all_to_all(plane, ("ylo", "x", "core"), split_axis=0, concat_axis=0, tiled=True)
    mine = collect(parts)
    other = lax.ppermute(mine, "yhi", [(0, 1), (1, 0)])
    return merge(place, mine, other)


def solution(mesh):
    fine = Mesh(mesh.devices.reshape(16, 2, 4, 2, 2), AXES)
    columns = ("ylo", "x", "core")
    return jax.shard_map(
        body,
        mesh=fine,
        in_specs=(P("yhi", ("z",) + columns, None), P(), P(), P(), P("yhi"), P(), P()),
        out_specs=P("z", columns),
        check_vma=False,
    )
```

```python
import jax
import jax.numpy as jnp
from jax import lax
from jax.experimental import pallas as pl
from jax.experimental.pallas import tpu as pltpu
from jax.sharding import Mesh
from jax.sharding import PartitionSpec as P

AXES = ("z", "ylo", "x", "core", "yhi")
Y_RING = ("ylo", "core", "yhi")
VMEM_LIMIT = 56 * 1024 * 1024
CHUNKS = 1
SCALE = 5e5
FLIPS = ((0, 0), (0, 1), (1, 0), (1, 1))


def lookup(table, indices):
    positions = jnp.arange(table.shape[0], dtype=jnp.int32)
    hits = indices[:, None] == positions[None, :]
    return jnp.sum(jnp.where(hits, table[None, :], jnp.float32(0.0)), axis=1)


def pack_kernel(src, *dst):
    width = dst[0].shape[2]
    for w in range(src.shape[0]):
        for half in range(2):
            for chunk in range(len(dst)):
                start = (half * len(dst) + chunk) * width
                dst[chunk][2 * w + half] = src[w, :, start : start + width]


def pack(factors):
    orbitals, rows, virt = factors.shape
    whole = pl.BlockSpec(memory_space=pltpu.VMEM)
    shape = jax.ShapeDtypeStruct((2 * orbitals, rows, virt // (2 * CHUNKS)), factors.dtype)
    return pl.pallas_call(
        pack_kernel,
        in_specs=[whole],
        out_specs=[whole] * CHUNKS,
        out_shape=[shape] * CHUNKS,
    )(factors)


def product_kernel(place, weight, p0, p1, p3, p2_low, p2_high, *refs):
    q_blocks = refs[:4]
    keep, send, left, right = refs[4:]
    step = pl.program_id(0)
    x, ylo, yhi, core = place[0], place[1], place[2], place[3]
    planes, depth = left.shape[0], left.shape[3]

    @pl.when(step == 0)
    def _():
        for shift, block, low, high in (
            (0, p0, 0, planes),
            (1, p1, 0, planes),
            (3, p3, 0, planes),
            (2, p2_low, 0, planes // 2),
            (2, p2_high, planes // 2, planes),
        ):
            at = lax.rem(x + 4 - shift, 4)

            def scale(r, carry, block=block, at=at, low=low):
                chunk = block[pl.ds(pl.multiple_of((r - low) * 16, 16), 16), :]
                left[r, at] = (chunk.astype(jnp.float32) * weight[...]).astype(jnp.bfloat16)
                return carry

            lax.fori_loop(low, high, scale, 0)
        for (s, t), block in zip(FLIPS, q_blocks):
            at = (ylo ^ t) * 2 + (yhi ^ s)

            def move(r, carry, block=block, at=at):
                right[r, at] = block[pl.ds(pl.multiple_of(r * 16, 16), 16), :]
                return carry

            lax.fori_loop(0, planes, move, 0)

    columns = right[pl.ds(step * 4, 4)].reshape(256, depth)
    low = lax.broadcasted_iota(jnp.int32, (32, 128), 1) < 64
    total = lax.dot_general(
        left[...].reshape(planes * 64, depth),
        columns,
        (((1,), (1,)), ((), ())),
        preferred_element_type=jnp.float32,
    )
    for r in range(planes):
        for pair in range(2):
            lanes = slice(pair * 128, pair * 128 + 128)
            top = total[r * 64 : r * 64 + 32, lanes]
            bottom = total[r * 64 + 32 : r * 64 + 64, lanes]
            even = jnp.where(low, top, pltpu.roll(bottom, 64, 1))
            odd = jnp.where(low, pltpu.roll(top, 64, 1), bottom)
            for at, both in ((2 * pair, even), (2 * pair + 1, odd)):
                keep[r, at] = jnp.where(core == 0, both[:16], both[16:])
                send[r, at] = jnp.where(core == 0, both[16:], both[:16])


def product(place, weight, p_blocks, q_blocks):
    rows, depth = p_blocks[0].shape
    whole = pl.BlockSpec(memory_space=pltpu.VMEM)
    part = pl.BlockSpec((16, 4, 16, 128), lambda n: (0, n, 0, 0))
    return pl.pallas_call(
        product_kernel,
        grid=(4,),
        in_specs=[pl.BlockSpec(memory_space=pltpu.SMEM)] + [whole] * 10,
        out_specs=[part] * 2,
        out_shape=[jax.ShapeDtypeStruct((16, 16, 16, 128), jnp.float32)] * 2,
        scratch_shapes=[pltpu.VMEM((rows // 16, 4, 16, depth), jnp.bfloat16)] * 2,
        compiler_params=pltpu.CompilerParams(vmem_limit_bytes=VMEM_LIMIT),
        cost_estimate=pl.CostEstimate(
            flops=2 * 1024 * 1024 * depth, bytes_accessed=10 * 1024 * 1024, transcendentals=0
        ),
    )(place, weight, *p_blocks, *q_blocks)


def collect_kernel(parts, out):
    lane = lax.broadcasted_iota(jnp.int32, (16, 128), 1) // 32
    for ylo in range(2):
        for core in range(2):
            for high in range(2):
                for column in range(2):
                    start = high * 64 + column * 32
                    total = jnp.zeros((16, 128), jnp.float32)
                    for x in range(4):
                        shift = (x * 32 - start) % 128
                        part = parts[ylo * 8 + x * 2 + core]
                        total = jnp.where(lane == x, pltpu.roll(part, shift, 1) if shift else part, total)
                    out[ylo * 4 + high * 2 + core, :, column * 128 : column * 128 + 128] = total


def collect(parts):
    return pl.pallas_call(
        collect_kernel, out_shape=jax.ShapeDtypeStruct((8, 16, 256), jnp.float32)
    )(parts)


def merge_kernel(place, mine, other, out):
    yhi = place[2]
    for group in range(8):
        a, b = mine[group], other[group]
        out[pl.ds(group * 32, 16), :] = jnp.where(yhi == 0, a, b)
        out[pl.ds(group * 32 + 16, 16), :] = jnp.where(yhi == 0, b, a)


def merge(place, mine, other):
    whole = pl.BlockSpec(memory_space=pltpu.VMEM)
    return pl.pallas_call(
        merge_kernel,
        in_specs=[pl.BlockSpec(memory_space=pltpu.SMEM), whole, whole],
        out_specs=whole,
        out_shape=jax.ShapeDtypeStruct((256, 256), jnp.float32),
    )(place, mine, other)


def ring_permutation(s, t):
    index = lambda ylo, core, yhi: (ylo * 2 + core) * 2 + yhi
    return [
        (index(ylo, core, yhi), index(ylo ^ t, yhi, core ^ s))
        for ylo in range(2)
        for core in range(2)
        for yhi in range(2)
    ]


def body(factors, occ_energies, virt_energies, freq_grid, occ_index, virt_index, freq_index):
    z, ylo, x, core, yhi = (lax.axis_index(a) for a in AXES)
    place = jnp.stack([x, ylo, yhi, core]).astype(jnp.int32)
    own_index = lax.ppermute(occ_index, Y_RING, ring_permutation(0, 0))
    chunks = [
        lax.all_to_all(chunk, "z", split_axis=0, concat_axis=0, tiled=True) for chunk in pack(factors)
    ]
    depth = chunks[0].shape[2]
    half = depth * CHUNKS

    own_virtual = lax.dynamic_slice_in_dim(virt_index, (z % 2) * half, half)
    own_occupied = lax.dynamic_slice_in_dim(own_index, z // 2, 1)
    excitation = lookup(virt_energies, own_virtual) - lookup(occ_energies, own_occupied)
    frequency = lookup(freq_grid, freq_index)[0]
    weight = -4.0 * excitation / (excitation * excitation + frequency * frequency)

    rows = chunks[0].reshape(-1, depth)
    q_blocks = [lax.ppermute(rows, Y_RING, ring_permutation(s, t)) for s, t in FLIPS]
    own = q_blocks[0]
    up = lambda block: lax.ppermute(block, "x", [(i, (i + 1) % 4) for i in range(4)])
    down = lambda block: lax.ppermute(block, "x", [(i, (i + 3) % 4) for i in range(4)])
    below, above = up(own), down(own)
    middle = own.shape[0] // 2
    p_blocks = [own, below, above, up(below[:middle]), down(above[middle:])]
    keep, send = product(place, weight[None, :], p_blocks, q_blocks)
    total = keep + lax.ppermute(send, "core", [(0, 1), (1, 0)])
    root = jnp.sqrt(jnp.abs(total) * SCALE)
    coded = jnp.where(total < 0, -root, root).astype(jnp.float16)
    terms = lax.all_to_all(
        coded.reshape(256, 16, 128), ("z", "ylo", "x", "core"), split_axis=0, concat_axis=0, tiled=True
    )
    terms = terms.reshape(16, 16, 16, 128).astype(jnp.float32)
    parts = jnp.sum(terms * jnp.abs(terms), axis=0) * (1.0 / SCALE)
    mine = collect(parts)
    other = lax.ppermute(mine, "yhi", [(0, 1), (1, 0)])
    return merge(place, mine, other)


def solution(mesh):
    fine = Mesh(mesh.devices.reshape(16, 2, 4, 2, 2), AXES)
    columns = ("ylo", "x", "core")
    return jax.shard_map(
        body,
        mesh=fine,
        in_specs=(P("yhi", ("z",) + columns, None), P(), P(), P(), P("yhi"), P(), P()),
        out_specs=P("z", columns),
        check_vma=False,
    )
```

```python
import jax
import jax.numpy as jnp
from jax import lax
from jax.experimental import pallas as pl
from jax.experimental.pallas import tpu as pltpu
from jax.sharding import Mesh
from jax.sharding import PartitionSpec as P

AXES = ("z", "ylo", "x", "core", "yhi")
Y_RING = ("ylo", "core", "yhi")
VMEM_LIMIT = 32 * 1024 * 1024
SHIFTS = 3
SCALE = 5e5
FLIPS = ((0, 0), (0, 1), (1, 0), (1, 1))


def lookup(table, indices):
    positions = jnp.arange(table.shape[0], dtype=jnp.int32)
    hits = indices[:, None] == positions[None, :]
    return jnp.sum(jnp.where(hits, table[None, :], jnp.float32(0.0)), axis=1)


def pack_kernel(src, dst):
    width = dst.shape[2]
    for w in range(src.shape[0]):
        for half in range(2):
            dst[2 * w + half] = src[w, :, half * width : half * width + width]


def pack(factors):
    orbitals, rows, virt = factors.shape
    whole = pl.BlockSpec(memory_space=pltpu.VMEM)
    return pl.pallas_call(
        pack_kernel,
        in_specs=[whole],
        out_specs=whole,
        out_shape=jax.ShapeDtypeStruct((2 * orbitals, rows, virt // 2), factors.dtype),
    )(factors)


def product_kernel(place, weight, p0, p1, p2, q00, q01, q10, q11, keep, send, left, right):
    ylo, yhi, core = place[0], place[1], place[2]
    planes, _, _, depth = right.shape

    for shift, block in enumerate((p0, p1, p2)):

        def scale(r, carry, block=block, shift=shift):
            chunk = block[pl.ds(pl.multiple_of(r * 16, 16), 16), :]
            left[r, shift] = (chunk.astype(jnp.float32) * weight[...]).astype(jnp.bfloat16)
            return carry

        lax.fori_loop(0, planes, scale, 0)
    for (s, t), block in zip(FLIPS, (q00, q01, q10, q11)):
        at = (ylo ^ t) * 2 + (yhi ^ s)

        def move(r, carry, block=block, at=at):
            right[r, at] = block[pl.ds(pl.multiple_of(r * 16, 16), 16), :]
            return carry

        lax.fori_loop(0, planes, move, 0)

    low = lax.broadcasted_iota(jnp.int32, (8, 128), 1) < 64

    def columns(step, carry):
        total = lax.dot_general(
            left[...].reshape(planes * SHIFTS * 16, depth),
            right[pl.ds(step * 4, 4)].reshape(256, depth),
            (((1,), (1,)), ((), ())),
            preferred_element_type=jnp.float32,
        )
        for r in range(planes):
            for pair in range(2):
                for shift in range(SHIFTS):
                    start = (r * SHIFTS + shift) * 16
                    tiles = total[start : start + 16, pair * 128 : pair * 128 + 128]
                    for ref, tile in (
                        (keep, jnp.where(core == 0, tiles[:8], tiles[8:])),
                        (send, jnp.where(core == 0, tiles[8:], tiles[:8])),
                    ):
                        turned = pltpu.roll(tile, 64, 1)
                        even = jnp.where(low, tile, pltpu.roll(turned, 4, 0))
                        odd = jnp.where(low, turned, pltpu.roll(tile, 4, 0))
                        lanes = slice(shift * 128, shift * 128 + 128)
                        ref[r, step * 4 + pair * 2, :, lanes] = even[:4]
                        ref[r, step * 4 + pair * 2 + 1, :, lanes] = odd[:4]
        return carry

    lax.fori_loop(0, 4, columns, 0)


def product(place, weight, p_blocks, q_blocks):
    rows, depth = p_blocks[0].shape
    planes = rows // 16
    whole = pl.BlockSpec(memory_space=pltpu.VMEM)
    return pl.pallas_call(
        product_kernel,
        in_specs=[pl.BlockSpec(memory_space=pltpu.SMEM)] + [whole] * 8,
        out_specs=[whole] * 2,
        out_shape=[jax.ShapeDtypeStruct((planes, planes, 4, SHIFTS * 128), jnp.float32)] * 2,
        scratch_shapes=[
            pltpu.VMEM((planes, SHIFTS, 16, depth), jnp.bfloat16),
            pltpu.VMEM((planes, 4, 16, depth), jnp.bfloat16),
        ],
        compiler_params=pltpu.CompilerParams(vmem_limit_bytes=VMEM_LIMIT),
        cost_estimate=pl.CostEstimate(
            flops=2 * SHIFTS * 256 * 1024 * depth, bytes_accessed=8 * 1024 * 1024, transcendentals=0
        ),
    )(place, weight, *p_blocks, *q_blocks)


def assemble_kernel(place, mine, other, mirror_mine, mirror_other, out, mirror):
    first = place[1] == 0
    lane = lax.broadcasted_iota(jnp.int32, (4, 128), 1) // 32

    def fill(target, pair, shifts, offset):
        for a in range(2):
            for ylo in range(2):
                for row_x in range(4):
                    for core in range(2):
                        for half in range(2):
                            for column in range(2):
                                start = half * 64 + column * 32
                                total = jnp.zeros((4, 128), jnp.float32)
                                for shift in shifts:
                                    x = (row_x + shift) % 4
                                    lanes = slice((shift - offset) * 128, (shift - offset) * 128 + 128)
                                    at = ylo * 8 + x * 2 + core
                                    part = jnp.where(first == (a == 0), pair[0][at, :, lanes], pair[1][at, :, lanes])
                                    turn = (x * 32 - start) % 128
                                    part = pltpu.roll(part, turn, 1) if turn else part
                                    total = jnp.where(lane == x, part, total)
                                row = (ylo * 8 + row_x * 2 + a) * 16 + core * 8 + half * 4
                                target[pl.ds(row, 4), column * 128 : column * 128 + 128] = total

    fill(out, (mine, other), (0, 1, 2), 0)
    fill(mirror, (mirror_mine, mirror_other), (1,), 1)
    x_of = lambda axis: (lax.broadcasted_iota(jnp.int32, out.shape, axis) // 32) % 4
    mirrored = (x_of(1) - x_of(0) + 4) % 4 == 3
    out[...] = jnp.where(mirrored, mirror[...].T, out[...])


def assemble(place, *parts):
    whole = pl.BlockSpec(memory_space=pltpu.VMEM)
    return pl.pallas_call(
        assemble_kernel,
        in_specs=[pl.BlockSpec(memory_space=pltpu.SMEM)] + [whole] * 4,
        out_specs=whole,
        out_shape=jax.ShapeDtypeStruct((256, 256), jnp.float32),
        scratch_shapes=[pltpu.VMEM((256, 256), jnp.float32)],
    )(place, *parts)


def ring_permutation(s, t):
    index = lambda ylo, core, yhi: (ylo * 2 + core) * 2 + yhi
    return [
        (index(ylo, core, yhi), index(ylo ^ t, yhi, core ^ s))
        for ylo in range(2)
        for core in range(2)
        for yhi in range(2)
    ]


def transposed(yhi_flip):
    index = lambda z, c, yhi: (z * 16 + c) * 2 + yhi
    return [
        (index(z, c, yhi), index(c, z, yhi ^ yhi_flip))
        for z in range(16)
        for c in range(16)
        for yhi in range(2)
    ]


def body(factors, occ_energies, virt_energies, freq_grid, occ_index, virt_index, freq_index):
    z, ylo, x, core, yhi = (lax.axis_index(a) for a in AXES)
    place = jnp.stack([ylo, yhi, core]).astype(jnp.int32)
    own_index = lax.ppermute(occ_index, Y_RING, ring_permutation(0, 0))
    planes = lax.all_to_all(pack(factors), "z", split_axis=0, concat_axis=0, tiled=True)
    depth = planes.shape[2]
    rows = planes.reshape(-1, depth)

    own_virtual = lax.dynamic_slice_in_dim(virt_index, (z % 2) * depth, depth)
    own_occupied = lax.dynamic_slice_in_dim(own_index, z // 2, 1)
    excitation = lookup(virt_energies, own_virtual) - lookup(occ_energies, own_occupied)
    frequency = lookup(freq_grid, freq_index)[0]
    weight = -4.0 * excitation / (excitation * excitation + frequency * frequency)

    q_blocks = [lax.ppermute(rows, Y_RING, ring_permutation(s, t)) for s, t in FLIPS]
    own = q_blocks[0]
    p_blocks = [own] + [
        lax.ppermute(own, "x", [(i, (i + shift) % 4) for i in range(4)]) for shift in range(1, SHIFTS)
    ]
    keep, send = product(place, weight[None, :], p_blocks, q_blocks)
    total = keep + lax.ppermute(send, "core", [(0, 1), (1, 0)])
    root = jnp.sqrt(jnp.abs(total) * SCALE)
    coded = jnp.where(total < 0, -root, root).astype(jnp.float16)
    coded = coded.reshape(256, 4, SHIFTS * 128)
    terms = lax.all_to_all(coded, ("z", "ylo", "x", "core"), split_axis=0, concat_axis=0, tiled=True)
    terms = terms.reshape(16, 16, 4, SHIFTS * 128).astype(jnp.float32)
    mine = jnp.sum(terms * jnp.abs(terms), axis=0) * (1.0 / SCALE)
    first_shift = mine[:, :, 128:256]
    other = lax.ppermute(mine, "yhi", [(0, 1), (1, 0)])
    mirror_mine = lax.ppermute(first_shift, AXES, transposed(0))
    mirror_other = lax.ppermute(first_shift, AXES, transposed(1))
    return assemble(place, mine, other, mirror_mine, mirror_other)


def solution(mesh):
    fine = Mesh(mesh.devices.reshape(16, 2, 4, 2, 2), AXES)
    columns = ("ylo", "x", "core")
    return jax.shard_map(
        body,
        mesh=fine,
        in_specs=(P("yhi", ("z",) + columns, None), P(), P(), P(), P("yhi"), P(), P()),
        out_specs=P("z", columns),
        check_vma=False,
    )
```

```python
import jax
import jax.numpy as jnp
from jax import lax
from jax.experimental import pallas as pl
from jax.experimental.pallas import tpu as pltpu
from jax.sharding import Mesh
from jax.sharding import PartitionSpec as P

AXES = ("z", "ylo", "x", "core", "yhi")
Y_RING = ("ylo", "core", "yhi")
VMEM_LIMIT = 32 * 1024 * 1024
SMALL_VMEM = 8 * 1024 * 1024
SHIFT_TILES = (0, 1, 3, 2)
SCALE = 5e5
FLIPS = ((0, 0), (0, 1), (1, 0), (1, 1))


def weight_kernel(occ_index, occ, freq, freq_index, virt, index, after, out):
    del after
    z = lax.axis_index("z")
    hits = index[...]
    lanes, groups = hits & 127, hits >> 7
    level = jnp.zeros(hits.shape, jnp.float32)
    for group in range(virt.shape[0]):
        table = jnp.broadcast_to(virt[group : group + 1, :], hits.shape)
        found = jnp.take_along_axis(table, lanes, axis=1, mode="promise_in_bounds")
        level = jnp.where(groups == group, found, level)
    excitation = level - occ[occ_index[z // 2]]
    frequency = freq[freq_index[0]]
    weight = -4.0 * excitation / (excitation * excitation + frequency * frequency)
    half = hits.shape[0] // 2
    weight = jnp.where(z % 2 == 0, weight[:half], weight[half:])
    for group in range(half):
        out[:, group * 128 : group * 128 + 128] = weight[group : group + 1]


def weights(occ_index, occ, freq, freq_index, virt, index, after):
    scalar, whole = pl.BlockSpec(memory_space=pltpu.SMEM), pl.BlockSpec(memory_space=pltpu.VMEM)
    return pl.pallas_call(
        weight_kernel,
        in_specs=[scalar] * 4 + [whole] * 3,
        out_specs=whole,
        out_shape=jax.ShapeDtypeStruct((1, index.shape[0] // 2), jnp.float32),
        compiler_params=pltpu.CompilerParams(vmem_limit_bytes=SMALL_VMEM),
        cost_estimate=pl.CostEstimate(flops=1, bytes_accessed=1, transcendentals=0),
    )(occ_index, occ, freq, freq_index, virt.reshape(-1, 128), index.reshape(-1, 128), after)


def pack_kernel(src, dst):
    width = dst.shape[2]
    for w in range(src.shape[0]):
        for half in range(2):
            dst[2 * w + half] = src[w, :, half * width : half * width + width]


def pack(factors):
    orbitals, rows, virt = factors.shape
    whole = pl.BlockSpec(memory_space=pltpu.VMEM)
    return pl.pallas_call(
        pack_kernel,
        in_specs=[whole],
        out_specs=whole,
        out_shape=jax.ShapeDtypeStruct((2 * orbitals, rows, virt // 2), factors.dtype),
        compiler_params=pltpu.CompilerParams(vmem_limit_bytes=SMALL_VMEM),
    )(factors)


def scaled_rows(left, shift, weight, blocks):
    first = 0
    for block in blocks:

        def scale(r, carry, block=block, first=first):
            chunk = block[pl.ds(pl.multiple_of(r * 16, 16), 16), :]
            left[first + r, shift] = (chunk.astype(jnp.float32) * weight[...]).astype(jnp.bfloat16)
            return carry

        count = block.shape[0] // 16
        lax.fori_loop(0, count, scale, 0)
        first += count


def multiply(left, right, keep, send, first):
    core = lax.axis_index("core")
    planes, shifts, _, depth = left.shape
    low = lax.broadcasted_iota(jnp.int32, (8, 128), 1) < 64

    def columns(step, carry):
        total = lax.dot_general(
            left[...].reshape(planes * shifts * 16, depth),
            right[pl.ds(step * 4, 4)].reshape(256, depth),
            (((1,), (1,)), ((), ())),
            preferred_element_type=jnp.float32,
        )
        for r in range(planes):
            for pair in range(2):
                for shift in range(shifts):
                    start = (r * shifts + shift) * 16
                    tiles = total[start : start + 16, pair * 128 : pair * 128 + 128]
                    for ref, tile in (
                        (keep, jnp.where(core == 0, tiles[:8], tiles[8:])),
                        (send, jnp.where(core == 0, tiles[8:], tiles[:8])),
                    ):
                        turned = pltpu.roll(tile, 64, 1)
                        even = jnp.where(low, tile, pltpu.roll(turned, 4, 0))
                        odd = jnp.where(low, turned, pltpu.roll(tile, 4, 0))
                        lanes = slice((first + shift) * 128, (first + shift) * 128 + 128)
                        ref[r, step * 4 + pair * 2, :, lanes] = even[:4]
                        ref[r, step * 4 + pair * 2 + 1, :, lanes] = odd[:4]
        return carry

    lax.fori_loop(0, 4, columns, 0)


def early_kernel(weight, p0, p1, p3, q00, q01, q10, q11, keep, send, right, left):
    ylo, yhi = lax.axis_index("ylo"), lax.axis_index("yhi")
    planes = right.shape[0]
    for (s, t), block in zip(FLIPS, (q00, q01, q10, q11)):
        at = (ylo ^ t) * 2 + (yhi ^ s)

        def move(r, carry, block=block, at=at):
            right[r, at] = block[pl.ds(pl.multiple_of(r * 16, 16), 16), :]
            return carry

        lax.fori_loop(0, planes, move, 0)
    for shift, block in enumerate((p0, p1, p3)):
        scaled_rows(left, shift, weight, (block,))
    multiply(left, right, keep, send, 0)


def late_kernel(weight, p2, right, keep_in, send_in, keep, send, left):
    del keep_in, send_in
    scaled_rows(left, 0, weight, (p2,))
    multiply(left, right, keep, send, 3)


def product(kernel, shifts, weight, *blocks):
    depth = blocks[0].shape[1]
    planes = 16
    whole = pl.BlockSpec(memory_space=pltpu.VMEM)
    packed = jax.ShapeDtypeStruct((planes, 4, 16, depth), jnp.bfloat16)
    results = [jax.ShapeDtypeStruct((planes, planes, 4, 512), jnp.float32)] * 2
    aliases = {}
    if kernel is early_kernel:
        results.append(packed)
    else:
        aliases = {len(blocks) - 1: 0, len(blocks): 1}
    return pl.pallas_call(
        kernel,
        in_specs=[whole] * (1 + len(blocks)),
        out_specs=[whole] * len(results),
        out_shape=results,
        scratch_shapes=[pltpu.VMEM((planes, shifts, 16, depth), jnp.bfloat16)],
        input_output_aliases=aliases,
        compiler_params=pltpu.CompilerParams(vmem_limit_bytes=VMEM_LIMIT),
        cost_estimate=pl.CostEstimate(
            flops=1, bytes_accessed=1, transcendentals=0
        ),
    )(weight, *blocks)


def assemble_kernel(mine, other, out):
    first = lax.axis_index("yhi") == 0
    lane = lax.broadcasted_iota(jnp.int32, (4, 128), 1) // 32
    for a in range(2):
        for ylo in range(2):
            for row_x in range(4):
                for core in range(2):
                    for half in range(2):
                        for column in range(2):
                            start = half * 64 + column * 32
                            total = jnp.zeros((4, 128), jnp.float32)
                            for x in range(4):
                                shift = (x - row_x) % 4
                                tile = SHIFT_TILES[shift]
                                lanes = slice(tile * 128, tile * 128 + 128)
                                at = ylo * 8 + x * 2 + core
                                part = jnp.where(first == (a == 0), mine[at, :, lanes], other[at, :, lanes])
                                turn = (x * 32 - start) % 128
                                part = pltpu.roll(part, turn, 1) if turn else part
                                total = jnp.where(lane == x, part, total)
                            row = (ylo * 8 + row_x * 2 + a) * 16 + core * 8 + half * 4
                            out[pl.ds(row, 4), column * 128 : column * 128 + 128] = total


def assemble(mine, other):
    whole = pl.BlockSpec(memory_space=pltpu.VMEM)
    return pl.pallas_call(
        assemble_kernel,
        in_specs=[whole] * 2,
        out_specs=whole,
        out_shape=jax.ShapeDtypeStruct((256, 256), jnp.float32),
        compiler_params=pltpu.CompilerParams(vmem_limit_bytes=SMALL_VMEM),
    )(mine, other)


def ring_permutation(s, t):
    index = lambda ylo, core, yhi: (ylo * 2 + core) * 2 + yhi
    return [
        (index(ylo, core, yhi), index(ylo ^ t, yhi, core ^ s))
        for ylo in range(2)
        for core in range(2)
        for yhi in range(2)
    ]


def flip_permutation(s, t):
    index = lambda ylo, core, yhi: (ylo * 2 + core) * 2 + yhi
    return [
        (index(ylo, core, yhi), index(ylo ^ t, core, yhi ^ s))
        for ylo in range(2)
        for core in range(2)
        for yhi in range(2)
    ]


def body(factors, occ_energies, virt_energies, freq_grid, occ_index, virt_index, freq_index):
    planes = lax.all_to_all(pack(factors), "z", split_axis=0, concat_axis=0, tiled=True)
    rows = planes.reshape(-1, planes.shape[2])

    own = lax.ppermute(rows, Y_RING, ring_permutation(0, 0))
    up = lambda block: lax.ppermute(block, "x", [(i, (i + 1) % 4) for i in range(4)])
    down = lambda block: lax.ppermute(block, "x", [(i, (i + 3) % 4) for i in range(4)])
    below, above = up(own), down(own)
    opposite = [lax.ppermute(own, "x", [(i, (i + 2) % 4) for i in range(4)])]
    q_blocks = [
        own,
        lax.ppermute(own, Y_RING, flip_permutation(0, 1)),
        lax.ppermute(rows, Y_RING, ring_permutation(1, 0)),
        lax.ppermute(own, Y_RING, flip_permutation(1, 1)),
    ]
    weight = weights(occ_index, occ_energies, freq_grid, freq_index, virt_energies, virt_index, rows)
    weight = lax.ppermute(weight, Y_RING, ring_permutation(0, 0))

    keep, send, right = product(early_kernel, 3, weight, own, below, above, *q_blocks)
    keep, send = product(late_kernel, 1, weight, *opposite, right, keep, send)
    total = keep + lax.ppermute(send, "core", [(0, 1), (1, 0)])
    root = jnp.sqrt(jnp.abs(total) * SCALE)
    coded = jnp.where(total < 0, -root, root).astype(jnp.float16)
    coded = coded.reshape(256, 4, 512)
    terms = lax.all_to_all(coded, ("z", "ylo", "x", "core"), split_axis=0, concat_axis=0, tiled=True)
    terms = terms.reshape(16, 16, 4, 512).astype(jnp.float32)
    mine = jnp.sum(terms * jnp.abs(terms), axis=0) * (1.0 / SCALE)
    other = lax.ppermute(mine, "yhi", [(0, 1), (1, 0)])
    return assemble(mine, other)


def solution(mesh):
    fine = Mesh(mesh.devices.reshape(16, 2, 4, 2, 2), AXES)
    columns = ("ylo", "x", "core")
    return jax.shard_map(
        body,
        mesh=fine,
        in_specs=(P("yhi", ("z",) + columns, None), P(), P(), P(), P("yhi"), P(), P()),
        out_specs=P("z", columns),
        check_vma=False,
    )
```

```python
import jax
import jax.numpy as jnp
from jax import lax
from jax.experimental import pallas as pl
from jax.experimental.pallas import tpu as pltpu
from jax.sharding import Mesh
from jax.sharding import PartitionSpec as P

AXES = ("z", "ylo", "x", "core", "yhi")
Y_RING = ("ylo", "core", "yhi")
VMEM_LIMIT = 12 * 1024 * 1024
SMALL_VMEM = 8 * 1024 * 1024
SHIFT_TILES = ((0, 0), (0, 1), (1, 1), (1, 0))
SCALE = 2.5e5
FLIPS = ((0, 0), (0, 1), (1, 0), (1, 1))


def weight_kernel(occ_index, occ, freq, freq_index, virt, index, after, out):
    del after
    z = lax.axis_index("z")
    hits = index[...]
    lanes, groups = hits & 127, hits >> 7
    level = jnp.zeros(hits.shape, jnp.float32)
    for group in range(virt.shape[0]):
        table = jnp.broadcast_to(virt[group : group + 1, :], hits.shape)
        found = jnp.take_along_axis(table, lanes, axis=1, mode="promise_in_bounds")
        level = jnp.where(groups == group, found, level)
    excitation = level - occ[occ_index[z // 2]]
    frequency = freq[freq_index[0]]
    weight = -4.0 * excitation / (excitation * excitation + frequency * frequency)
    half = hits.shape[0] // 2
    weight = jnp.where(z % 2 == 0, weight[:half], weight[half:])
    for group in range(half):
        out[:, group * 128 : group * 128 + 128] = weight[group : group + 1]


def weights(occ_index, occ, freq, freq_index, virt, index, after):
    scalar, whole = pl.BlockSpec(memory_space=pltpu.SMEM), pl.BlockSpec(memory_space=pltpu.VMEM)
    return pl.pallas_call(
        weight_kernel,
        in_specs=[scalar] * 4 + [whole] * 3,
        out_specs=whole,
        out_shape=jax.ShapeDtypeStruct((1, index.shape[0] // 2), jnp.float32),
        compiler_params=pltpu.CompilerParams(vmem_limit_bytes=SMALL_VMEM),
        cost_estimate=pl.CostEstimate(flops=1, bytes_accessed=1, transcendentals=0),
    )(occ_index, occ, freq, freq_index, virt.reshape(-1, 128), index.reshape(-1, 128), after)


def pack_kernel(src, dst):
    width = dst.shape[2]
    for w in range(src.shape[0]):
        for half in range(2):
            dst[2 * w + half] = src[w, :, half * width : half * width + width]


def pack(factors):
    orbitals, rows, virt = factors.shape
    whole = pl.BlockSpec(memory_space=pltpu.VMEM)
    return pl.pallas_call(
        pack_kernel,
        in_specs=[whole],
        out_specs=whole,
        out_shape=jax.ShapeDtypeStruct((2 * orbitals, rows, virt // 2), factors.dtype),
        compiler_params=pltpu.CompilerParams(vmem_limit_bytes=SMALL_VMEM),
    )(factors)


def scaled_rows(left, shift, weight, blocks):
    first = 0
    for block in blocks:

        def scale(r, carry, block=block, first=first):
            chunk = block[pl.ds(pl.multiple_of(r * 16, 16), 16), :]
            left[first + r, shift] = (chunk.astype(jnp.float32) * weight[...]).astype(jnp.bfloat16)
            return carry

        count = block.shape[0] // 16
        lax.fori_loop(0, count, scale, 0)
        first += count


def multiply(left, right, keep, send, shares):
    core = lax.axis_index("core")
    parity = lax.axis_index("z") % 2
    planes, shifts, _, depth = left.shape
    low = lax.broadcasted_iota(jnp.int32, (8, 128), 1) < 64
    top = lax.broadcasted_iota(jnp.int32, (8, 128), 0) < 4

    def columns(step, carry):
        total = lax.dot_general(
            left[...].reshape(planes * shifts * 16, depth),
            right[pl.ds(step * 4, 4)].reshape(256, depth),
            (((1,), (1,)), ((), ())),
            preferred_element_type=jnp.float32,
        )

        def tile(r, shift, pair, half):
            start = (r * shifts + shift) * 16
            tiles = total[start : start + 16, pair * 128 : pair * 128 + 128]
            return jnp.where(core == half, tiles[:8], tiles[8:])

        for r in range(planes):
            for pair in range(2):
                for share, (a, b) in shares.items():
                    for half, ref in ((0, keep), (1, send)):
                        if a is not None:
                            first = tile(r, a, pair, half)
                            first_turned = pltpu.roll(first, 64, 1)
                            even = jnp.where(low, first, pltpu.roll(first_turned, 4, 0))
                            odd = jnp.where(low, first_turned, pltpu.roll(first, 4, 0))
                            rows = slice(0, 4)
                        if b is not None:
                            second = tile(r, b, pair, half)
                            second_turned = pltpu.roll(second, 64, 1)
                            even_b = jnp.where(low, pltpu.roll(second, 4, 0), second_turned)
                            odd_b = jnp.where(low, pltpu.roll(second_turned, 4, 0), second)
                            rows = slice(4, 8)
                            if a is None:
                                even, odd = even_b, odd_b
                            else:
                                even, odd = jnp.where(top, even, even_b), jnp.where(top, odd, odd_b)
                                rows = slice(0, 8)
                        ref[share ^ parity, r, step * 4 + pair * 2, rows, :] = even[rows]
                        ref[share ^ parity, r, step * 4 + pair * 2 + 1, rows, :] = odd[rows]
        return carry

    lax.fori_loop(0, 4, columns, 0)


def early_kernel(weight, p0, p1, p3, q00, q01, q10, q11, keep, send, right, left):
    ylo, yhi = lax.axis_index("ylo"), lax.axis_index("yhi")
    planes = right.shape[0]
    for (s, t), block in zip(FLIPS, (q00, q01, q10, q11)):
        at = (ylo ^ t) * 2 + (yhi ^ s)

        def move(r, carry, block=block, at=at):
            right[r, at] = block[pl.ds(pl.multiple_of(r * 16, 16), 16), :]
            return carry

        lax.fori_loop(0, planes, move, 0)
    for shift, block in enumerate((p0, p1, p3)):
        scaled_rows(left, shift, weight, (block,))
    multiply(left, right, keep, send, {0: (0, 1), 1: (2, None)})


def late_kernel(weight, p2, right, keep_in, send_in, keep, send, left):
    del keep_in, send_in
    scaled_rows(left, 0, weight, (p2,))
    multiply(left, right, keep, send, {1: (None, 0)})


def product(kernel, shifts, weight, *blocks):
    depth = blocks[0].shape[1]
    planes = 16
    whole = pl.BlockSpec(memory_space=pltpu.VMEM)
    packed = jax.ShapeDtypeStruct((planes, 4, 16, depth), jnp.bfloat16)
    results = [jax.ShapeDtypeStruct((2, planes, planes, 8, 128), jnp.float32)] * 2
    aliases = {}
    if kernel is early_kernel:
        results.append(packed)
    else:
        aliases = {len(blocks) - 1: 0, len(blocks): 1}
    return pl.pallas_call(
        kernel,
        in_specs=[whole] * (1 + len(blocks)),
        out_specs=[whole] * len(results),
        out_shape=results,
        scratch_shapes=[pltpu.VMEM((planes, shifts, 16, depth), jnp.bfloat16)],
        input_output_aliases=aliases,
        compiler_params=pltpu.CompilerParams(vmem_limit_bytes=VMEM_LIMIT),
        cost_estimate=pl.CostEstimate(
            flops=1, bytes_accessed=1, transcendentals=0
        ),
    )(weight, *blocks)


def assemble_kernel(mine, other, out):
    first = lax.axis_index("yhi") == 0
    lane = lax.broadcasted_iota(jnp.int32, (4, 128), 1) // 32
    for a in range(2):
        for ylo in range(2):
            for row_x in range(4):
                for core in range(2):
                    for half in range(2):
                        for column in range(2):
                            start = half * 64 + column * 32
                            total = jnp.zeros((4, 128), jnp.float32)
                            for x in range(4):
                                shift = (x - row_x) % 4
                                share, tile = SHIFT_TILES[shift]
                                rows = slice(tile * 4, tile * 4 + 4)
                                at = ylo * 8 + x * 2 + core
                                part = jnp.where(first == (a == 0), mine[share, at, rows, :], other[share, at, rows, :])
                                turn = (x * 32 - start) % 128
                                part = pltpu.roll(part, turn, 1) if turn else part
                                total = jnp.where(lane == x, part, total)
                            row = (ylo * 8 + row_x * 2 + a) * 16 + core * 8 + half * 4
                            out[pl.ds(row, 4), column * 128 : column * 128 + 128] = total


def assemble(mine, other):
    whole = pl.BlockSpec(memory_space=pltpu.VMEM)
    return pl.pallas_call(
        assemble_kernel,
        in_specs=[whole] * 2,
        out_specs=whole,
        out_shape=jax.ShapeDtypeStruct((256, 256), jnp.float32),
        compiler_params=pltpu.CompilerParams(vmem_limit_bytes=SMALL_VMEM),
    )(mine, other)


def ring_permutation(s, t):
    index = lambda ylo, core, yhi: (ylo * 2 + core) * 2 + yhi
    return [
        (index(ylo, core, yhi), index(ylo ^ t, yhi, core ^ s))
        for ylo in range(2)
        for core in range(2)
        for yhi in range(2)
    ]


def flip_permutation(s, t):
    index = lambda ylo, core, yhi: (ylo * 2 + core) * 2 + yhi
    return [
        (index(ylo, core, yhi), index(ylo ^ t, core, yhi ^ s))
        for ylo in range(2)
        for core in range(2)
        for yhi in range(2)
    ]


def encode(terms):
    root = jnp.sqrt(jnp.abs(terms) * SCALE)
    return jnp.where(terms < 0, -root, root).astype(jnp.float16)


def decode(codes):
    root = codes.astype(jnp.float32)
    return root * jnp.abs(root) * (1.0 / SCALE)


def body(factors, occ_energies, virt_energies, freq_grid, occ_index, virt_index, freq_index):
    planes = lax.all_to_all(pack(factors), "z", split_axis=0, concat_axis=0, tiled=True)
    rows = planes.reshape(-1, planes.shape[2])

    own = lax.ppermute(rows, Y_RING, ring_permutation(0, 0))
    up = lambda block: lax.ppermute(block, "x", [(i, (i + 1) % 4) for i in range(4)])
    down = lambda block: lax.ppermute(block, "x", [(i, (i + 3) % 4) for i in range(4)])
    below, above = up(own), down(own)
    opposite = [lax.ppermute(own, "x", [(i, (i + 2) % 4) for i in range(4)])]
    q_blocks = [
        own,
        lax.ppermute(own, Y_RING, flip_permutation(0, 1)),
        lax.ppermute(rows, Y_RING, ring_permutation(1, 0)),
        lax.ppermute(own, Y_RING, flip_permutation(1, 1)),
    ]
    weight = weights(occ_index, occ_energies, freq_grid, freq_index, virt_energies, virt_index, rows)
    weight = lax.ppermute(weight, Y_RING, ring_permutation(0, 0))

    keep, send, right = product(early_kernel, 3, weight, own, below, above, *q_blocks)
    keep, send = product(late_kernel, 1, weight, *opposite, right, keep, send)
    got = lax.ppermute(send, "core", [(0, 1), (1, 0)])
    passed = lax.ppermute(encode(keep[1] + got[1]), "z", [(i, i ^ 1) for i in range(16)])
    pairs = encode(keep[0] + got[0] + decode(passed))
    terms = lax.all_to_all(
        pairs.reshape(256, 8, 128), ("z", "ylo", "x", "core"), split_axis=0, concat_axis=0, tiled=True
    )
    mine = jnp.sum(decode(terms).reshape(8, 2, 16, 8, 128), axis=0)
    other = lax.ppermute(mine, "yhi", [(0, 1), (1, 0)])
    return assemble(mine, other)


def solution(mesh):
    fine = Mesh(mesh.devices.reshape(16, 2, 4, 2, 2), AXES)
    columns = ("ylo", "x", "core")
    return jax.shard_map(
        body,
        mesh=fine,
        in_specs=(P("yhi", ("z",) + columns, None), P(), P(), P(), P("yhi"), P(), P()),
        out_specs=P("z", columns),
        check_vma=False,
    )
```

```python
import jax
import jax.numpy as jnp
from jax import lax
from jax.experimental import pallas as pl
from jax.experimental.pallas import tpu as pltpu
from jax.sharding import Mesh
from jax.sharding import PartitionSpec as P

AXES = ("z", "ylo", "x", "core", "yhi")
Y_RING = ("ylo", "core", "yhi")
VMEM_LIMIT = 12 * 1024 * 1024
SMALL_VMEM = 8 * 1024 * 1024
SHIFT_TILES = ((0, 0), (0, 1), (1, 0), (1, 1))
SCALE = 2.5e5
FLIPS = ((0, 0), (0, 1), (1, 0), (1, 1))


def weight_kernel(occ_index, occ, freq, freq_index, virt, index, after, out):
    del after
    z = lax.axis_index("z")
    hits = index[...]
    lanes, groups = hits & 127, hits >> 7
    level = jnp.zeros(hits.shape, jnp.float32)
    for group in range(virt.shape[0]):
        table = jnp.broadcast_to(virt[group : group + 1, :], hits.shape)
        found = jnp.take_along_axis(table, lanes, axis=1, mode="promise_in_bounds")
        level = jnp.where(groups == group, found, level)
    excitation = level - occ[occ_index[z // 2]]
    frequency = freq[freq_index[0]]
    weight = -4.0 * excitation / (excitation * excitation + frequency * frequency)
    half = hits.shape[0] // 2
    weight = jnp.where(z % 2 == 0, weight[:half], weight[half:])
    for group in range(half):
        out[:, group * 128 : group * 128 + 128] = weight[group : group + 1]


def weights(occ_index, occ, freq, freq_index, virt, index, after):
    scalar, whole = pl.BlockSpec(memory_space=pltpu.SMEM), pl.BlockSpec(memory_space=pltpu.VMEM)
    return pl.pallas_call(
        weight_kernel,
        in_specs=[scalar] * 4 + [whole] * 3,
        out_specs=whole,
        out_shape=jax.ShapeDtypeStruct((1, index.shape[0] // 2), jnp.float32),
        compiler_params=pltpu.CompilerParams(vmem_limit_bytes=SMALL_VMEM),
        cost_estimate=pl.CostEstimate(flops=1, bytes_accessed=1, transcendentals=0),
    )(occ_index, occ, freq, freq_index, virt.reshape(-1, 128), index.reshape(-1, 128), after)


def pack_kernel(src, dst):
    width = dst.shape[2]
    for w in range(src.shape[0]):
        for half in range(2):
            dst[2 * w + half] = src[w, :, half * width : half * width + width]


def pack(factors):
    orbitals, rows, virt = factors.shape
    whole = pl.BlockSpec(memory_space=pltpu.VMEM)
    return pl.pallas_call(
        pack_kernel,
        in_specs=[whole],
        out_specs=whole,
        out_shape=jax.ShapeDtypeStruct((2 * orbitals, rows, virt // 2), factors.dtype),
        compiler_params=pltpu.CompilerParams(vmem_limit_bytes=SMALL_VMEM),
    )(factors)


def scaled_rows(left, shift, weight, blocks):
    first = 0
    for block in blocks:

        def scale(r, carry, block=block, first=first):
            chunk = block[pl.ds(pl.multiple_of(r * 16, 16), 16), :]
            left[first + r, shift] = (chunk.astype(jnp.float32) * weight[...]).astype(jnp.bfloat16)
            return carry

        count = block.shape[0] // 16
        lax.fori_loop(0, count, scale, 0)
        first += count


def multiply(left, right, keep, send, shares):
    core = lax.axis_index("core")
    parity = lax.axis_index("z") % 2
    planes, shifts, _, depth = left.shape
    low = lax.broadcasted_iota(jnp.int32, (8, 128), 1) < 64
    top = lax.broadcasted_iota(jnp.int32, (8, 128), 0) < 4

    def columns(step, carry):
        total = lax.dot_general(
            left[...].reshape(planes * shifts * 16, depth),
            right[pl.ds(step * 4, 4)].reshape(256, depth),
            (((1,), (1,)), ((), ())),
            preferred_element_type=jnp.float32,
        )

        def tile(r, shift, pair, half):
            start = (r * shifts + shift) * 16
            tiles = total[start : start + 16, pair * 128 : pair * 128 + 128]
            return jnp.where(core == half, tiles[:8], tiles[8:])

        for r in range(planes):
            for pair in range(2):
                for share, (a, b) in shares.items():
                    for half, ref in ((0, keep), (1, send)):
                        if a is not None:
                            first = tile(r, a, pair, half)
                            first_turned = pltpu.roll(first, 64, 1)
                            even = jnp.where(low, first, pltpu.roll(first_turned, 4, 0))
                            odd = jnp.where(low, first_turned, pltpu.roll(first, 4, 0))
                            rows = slice(0, 4)
                        if b is not None:
                            second = tile(r, b, pair, half)
                            second_turned = pltpu.roll(second, 64, 1)
                            even_b = jnp.where(low, pltpu.roll(second, 4, 0), second_turned)
                            odd_b = jnp.where(low, pltpu.roll(second_turned, 4, 0), second)
                            rows = slice(4, 8)
                            if a is None:
                                even, odd = even_b, odd_b
                            else:
                                even, odd = jnp.where(top, even, even_b), jnp.where(top, odd, odd_b)
                                rows = slice(0, 8)
                        ref[share ^ parity, r, step * 4 + pair * 2, rows, :] = even[rows]
                        ref[share ^ parity, r, step * 4 + pair * 2 + 1, rows, :] = odd[rows]
        return carry

    lax.fori_loop(0, 4, columns, 0)


def early_kernel(weight, p0, p1, p2, q00, q01, q10, q11, keep, send, right, left):
    ylo, yhi = lax.axis_index("ylo"), lax.axis_index("yhi")
    planes = right.shape[0]
    for (s, t), block in zip(FLIPS, (q00, q01, q10, q11)):
        at = (ylo ^ t) * 2 + (yhi ^ s)

        def move(r, carry, block=block, at=at):
            right[r, at] = block[pl.ds(pl.multiple_of(r * 16, 16), 16), :]
            return carry

        lax.fori_loop(0, planes, move, 0)
    for shift, block in enumerate((p0, p1, p2)):
        scaled_rows(left, shift, weight, (block,))
    multiply(left, right, keep, send, {0: (0, 1), 1: (2, None)})


def late_kernel(weight, p3, right, keep_in, send_in, keep, send, left):
    del keep_in, send_in
    scaled_rows(left, 0, weight, (p3,))
    multiply(left, right, keep, send, {1: (None, 0)})


def product(kernel, shifts, weight, *blocks):
    depth = blocks[0].shape[1]
    planes = 16
    whole = pl.BlockSpec(memory_space=pltpu.VMEM)
    packed = jax.ShapeDtypeStruct((planes, 4, 16, depth), jnp.bfloat16)
    results = [jax.ShapeDtypeStruct((2, planes, planes, 8, 128), jnp.float32)] * 2
    aliases = {}
    if kernel is early_kernel:
        results.append(packed)
    else:
        aliases = {len(blocks) - 1: 0, len(blocks): 1}
    return pl.pallas_call(
        kernel,
        in_specs=[whole] * (1 + len(blocks)),
        out_specs=[whole] * len(results),
        out_shape=results,
        scratch_shapes=[pltpu.VMEM((planes, shifts, 16, depth), jnp.bfloat16)],
        input_output_aliases=aliases,
        compiler_params=pltpu.CompilerParams(vmem_limit_bytes=VMEM_LIMIT),
        cost_estimate=pl.CostEstimate(
            flops=1, bytes_accessed=1, transcendentals=0
        ),
    )(weight, *blocks)


def assemble_kernel(mine, other, out):
    first = lax.axis_index("yhi") == 0
    lane = lax.broadcasted_iota(jnp.int32, (4, 128), 1) // 32
    for a in range(2):
        for ylo in range(2):
            for row_x in range(4):
                for core in range(2):
                    for half in range(2):
                        for column in range(2):
                            start = half * 64 + column * 32
                            total = jnp.zeros((4, 128), jnp.float32)
                            for x in range(4):
                                shift = (x - row_x) % 4
                                share, tile = SHIFT_TILES[shift]
                                rows = slice(tile * 4, tile * 4 + 4)
                                at = ylo * 8 + x * 2 + core
                                part = jnp.where(first == (a == 0), mine[share, at, rows, :], other[share, at, rows, :])
                                turn = (x * 32 - start) % 128
                                part = pltpu.roll(part, turn, 1) if turn else part
                                total = jnp.where(lane == x, part, total)
                            row = (ylo * 8 + row_x * 2 + a) * 16 + core * 8 + half * 4
                            out[pl.ds(row, 4), column * 128 : column * 128 + 128] = total


def assemble(mine, other):
    whole = pl.BlockSpec(memory_space=pltpu.VMEM)
    return pl.pallas_call(
        assemble_kernel,
        in_specs=[whole] * 2,
        out_specs=whole,
        out_shape=jax.ShapeDtypeStruct((256, 256), jnp.float32),
        compiler_params=pltpu.CompilerParams(vmem_limit_bytes=SMALL_VMEM),
    )(mine, other)


def ring_permutation(s, t):
    index = lambda ylo, core, yhi: (ylo * 2 + core) * 2 + yhi
    return [
        (index(ylo, core, yhi), index(ylo ^ t, yhi, core ^ s))
        for ylo in range(2)
        for core in range(2)
        for yhi in range(2)
    ]


def flip_permutation(s, t):
    index = lambda ylo, core, yhi: (ylo * 2 + core) * 2 + yhi
    return [
        (index(ylo, core, yhi), index(ylo ^ t, core, yhi ^ s))
        for ylo in range(2)
        for core in range(2)
        for yhi in range(2)
    ]


def neighbour_planes():
    other = lambda z, core: ((z + core) ^ 1) - core
    return [(z * 2 + core, other(z, core) % 16 * 2 + core) for z in range(16) for core in range(2)]


def encode(terms):
    root = jnp.sqrt(jnp.abs(terms) * SCALE)
    return jnp.where(terms < 0, -root, root).astype(jnp.float16)


def decode(codes):
    root = codes.astype(jnp.float32)
    return root * jnp.abs(root) * (1.0 / SCALE)


def body(factors, occ_energies, virt_energies, freq_grid, occ_index, virt_index, freq_index):
    planes = lax.all_to_all(pack(factors), "z", split_axis=0, concat_axis=0, tiled=True)
    rows = planes.reshape(-1, planes.shape[2])

    own = lax.ppermute(rows, Y_RING, ring_permutation(0, 0))
    step, opposite, back = [
        lax.ppermute(own, "x", [(i, (i + shift) % 4) for i in range(4)]) for shift in (1, 2, 3)
    ]
    q_blocks = [
        own,
        lax.ppermute(own, Y_RING, flip_permutation(0, 1)),
        lax.ppermute(rows, Y_RING, ring_permutation(1, 0)),
        lax.ppermute(own, Y_RING, flip_permutation(1, 1)),
    ]
    weight = weights(occ_index, occ_energies, freq_grid, freq_index, virt_energies, virt_index, rows)
    weight = lax.ppermute(weight, Y_RING, ring_permutation(0, 0))

    keep, send, right = product(early_kernel, 3, weight, own, step, opposite, *q_blocks)
    keep, send = product(late_kernel, 1, weight, back, right, keep, send)
    got = lax.ppermute(send, "core", [(0, 1), (1, 0)])
    passed = lax.ppermute(encode(keep[1] + got[1]), ("z", "core"), neighbour_planes())
    pairs = encode(keep[0] + got[0] + decode(passed))
    terms = lax.all_to_all(
        pairs.reshape(256, 8, 128), ("z", "ylo", "x", "core"), split_axis=0, concat_axis=0, tiled=True
    )
    mine = jnp.sum(decode(terms).reshape(8, 2, 16, 8, 128), axis=0)
    other = lax.ppermute(mine, "yhi", [(0, 1), (1, 0)])
    return assemble(mine, other)


def solution(mesh):
    fine = Mesh(mesh.devices.reshape(16, 2, 4, 2, 2), AXES)
    columns = ("ylo", "x", "core")
    return jax.shard_map(
        body,
        mesh=fine,
        in_specs=(P("yhi", ("z",) + columns, None), P(), P(), P(), P("yhi"), P(), P()),
        out_specs=P("z", columns),
        check_vma=False,
    )
```

```python
import jax
import jax.numpy as jnp
from jax import lax
from jax.experimental import pallas as pl
from jax.experimental.pallas import tpu as pltpu
from jax.sharding import Mesh
from jax.sharding import PartitionSpec as P

AXES = ("z", "ylo", "x", "core", "yhi")
Y_RING = ("ylo", "core", "yhi")
VMEM_LIMIT = 20 * 1024 * 1024
SMALL_VMEM = 8 * 1024 * 1024
SHIFT_TILES = ((0, 0), (0, 1), (1, 0), (1, 1))
SCALE = 2.5e5
FLIPS = ((0, 0), (0, 1), (1, 0), (1, 1))


def weight_kernel(occ_index, occ, freq, freq_index, virt, index, after, out):
    del after
    z = lax.axis_index("z")
    hits = index[...]
    lanes, groups = hits & 127, hits >> 7
    level = jnp.zeros(hits.shape, jnp.float32)
    for group in range(virt.shape[0]):
        table = jnp.broadcast_to(virt[group : group + 1, :], hits.shape)
        found = jnp.take_along_axis(table, lanes, axis=1, mode="promise_in_bounds")
        level = jnp.where(groups == group, found, level)
    excitation = level - occ[occ_index[z // 2]]
    frequency = freq[freq_index[0]]
    weight = -4.0 * excitation / (excitation * excitation + frequency * frequency)
    half = hits.shape[0] // 2
    weight = jnp.where(z % 2 == 0, weight[:half], weight[half:])
    for group in range(half):
        out[:, group * 128 : group * 128 + 128] = weight[group : group + 1]


def weights(occ_index, occ, freq, freq_index, virt, index, after):
    scalar, whole = pl.BlockSpec(memory_space=pltpu.SMEM), pl.BlockSpec(memory_space=pltpu.VMEM)
    return pl.pallas_call(
        weight_kernel,
        in_specs=[scalar] * 4 + [whole] * 3,
        out_specs=whole,
        out_shape=jax.ShapeDtypeStruct((1, index.shape[0] // 2), jnp.float32),
        compiler_params=pltpu.CompilerParams(vmem_limit_bytes=SMALL_VMEM),
        cost_estimate=pl.CostEstimate(flops=1, bytes_accessed=1, transcendentals=0),
    )(occ_index, occ, freq, freq_index, virt.reshape(-1, 128), index.reshape(-1, 128), after)


def pack_kernel(src, dst):
    width = dst.shape[2]
    for w in range(src.shape[0]):
        for half in range(2):
            dst[2 * w + half] = src[w, :, half * width : half * width + width]


def pack(factors):
    orbitals, rows, virt = factors.shape
    whole = pl.BlockSpec(memory_space=pltpu.VMEM)
    return pl.pallas_call(
        pack_kernel,
        in_specs=[whole],
        out_specs=whole,
        out_shape=jax.ShapeDtypeStruct((2 * orbitals, rows, virt // 2), factors.dtype),
        compiler_params=pltpu.CompilerParams(vmem_limit_bytes=SMALL_VMEM),
    )(factors)


def scaled_rows(left, shift, weight, blocks):
    first = 0
    for block in blocks:

        def scale(r, carry, block=block, first=first):
            chunk = block[pl.ds(pl.multiple_of(r * 16, 16), 16), :]
            left[first + r, shift] = (chunk.astype(jnp.float32) * weight[...]).astype(jnp.bfloat16)
            return carry

        count = block.shape[0] // 16
        lax.fori_loop(0, count, scale, 0)
        first += count


def multiply(left, right, keep, send, shares):
    core = lax.axis_index("core")
    parity = lax.axis_index("z") % 2
    planes, shifts, _, depth = left.shape
    low = lax.broadcasted_iota(jnp.int32, (8, 128), 1) < 64
    top = lax.broadcasted_iota(jnp.int32, (8, 128), 0) < 4

    def columns(step, carry):
        total = lax.dot_general(
            left[...].reshape(planes * shifts * 16, depth),
            right[pl.ds(step * 4, 4)].reshape(256, depth),
            (((1,), (1,)), ((), ())),
            preferred_element_type=jnp.float32,
        )

        def tile(r, shift, pair, half):
            start = (r * shifts + shift) * 16
            tiles = total[start : start + 16, pair * 128 : pair * 128 + 128]
            return jnp.where(core == half, tiles[:8], tiles[8:])

        for r in range(planes):
            for pair in range(2):
                for share, (a, b) in shares.items():
                    for half, ref in ((0, keep), (1, send)):
                        if a is not None:
                            first = tile(r, a, pair, half)
                            first_turned = pltpu.roll(first, 64, 1)
                            even = jnp.where(low, first, pltpu.roll(first_turned, 4, 0))
                            odd = jnp.where(low, first_turned, pltpu.roll(first, 4, 0))
                            rows = slice(0, 4)
                        if b is not None:
                            second = tile(r, b, pair, half)
                            second_turned = pltpu.roll(second, 64, 1)
                            even_b = jnp.where(low, pltpu.roll(second, 4, 0), second_turned)
                            odd_b = jnp.where(low, pltpu.roll(second_turned, 4, 0), second)
                            rows = slice(4, 8)
                            if a is None:
                                even, odd = even_b, odd_b
                            else:
                                even, odd = jnp.where(top, even, even_b), jnp.where(top, odd, odd_b)
                                rows = slice(0, 8)
                        ref[share ^ parity ^ core, r, step * 4 + pair * 2, rows, :] = even[rows]
                        ref[share ^ parity ^ core, r, step * 4 + pair * 2 + 1, rows, :] = odd[rows]
        return carry

    lax.fori_loop(0, 4, columns, 0)


def product_kernel(weight, p0, p3, q11, q10, q01, q00, p2, p1, keep, send, right, left):
    ylo, yhi = lax.axis_index("ylo"), lax.axis_index("yhi")
    planes = right.shape[0]
    for (s, t), block in zip(FLIPS, (q00, q01, q10, q11)):
        at = (ylo ^ t) * 2 + (yhi ^ s)

        def move(r, carry, block=block, at=at):
            right[r, at] = block[pl.ds(pl.multiple_of(r * 16, 16), 16), :]
            return carry

        lax.fori_loop(0, planes, move, 0)
    core = lax.axis_index("core")
    for slot, block in ((2 * core, p0), (1, p1), (2 - 2 * core, p2), (3, p3)):
        scaled_rows(left, slot, weight, (block,))
    multiply(left, right, keep, send, {0: (0, 1), 1: (2, 3)})


def product(weight, *blocks):
    depth = blocks[0].shape[1]
    whole = pl.BlockSpec(memory_space=pltpu.VMEM)
    return pl.pallas_call(
        product_kernel,
        in_specs=[whole] * 9,
        out_specs=[whole] * 2,
        out_shape=[jax.ShapeDtypeStruct((2, 16, 16, 8, 128), jnp.float32)] * 2,
        scratch_shapes=[pltpu.VMEM((16, 4, 16, depth), jnp.bfloat16)] * 2,
        compiler_params=pltpu.CompilerParams(vmem_limit_bytes=VMEM_LIMIT),
        cost_estimate=pl.CostEstimate(flops=1, bytes_accessed=1, transcendentals=0),
    )(weight, *blocks)


def assemble_kernel(mine, other, out):
    first = lax.axis_index("yhi") == 0
    lane = lax.broadcasted_iota(jnp.int32, (4, 128), 1) // 32
    for a in range(2):
        for ylo in range(2):
            for row_x in range(4):
                for core in range(2):
                    for half in range(2):
                        for column in range(2):
                            start = half * 64 + column * 32
                            total = jnp.zeros((4, 128), jnp.float32)
                            for x in range(4):
                                shift = (x - row_x) % 4
                                share, tile = SHIFT_TILES[shift]
                                rows = slice(tile * 4, tile * 4 + 4)
                                at = ylo * 8 + x * 2 + core
                                part = jnp.where(first == (a == 0), mine[share, at, rows, :], other[share, at, rows, :])
                                turn = (x * 32 - start) % 128
                                part = pltpu.roll(part, turn, 1) if turn else part
                                total = jnp.where(lane == x, part, total)
                            row = (ylo * 8 + row_x * 2 + a) * 16 + core * 8 + half * 4
                            out[pl.ds(row, 4), column * 128 : column * 128 + 128] = total


def assemble(mine, other):
    whole = pl.BlockSpec(memory_space=pltpu.VMEM)
    return pl.pallas_call(
        assemble_kernel,
        in_specs=[whole] * 2,
        out_specs=whole,
        out_shape=jax.ShapeDtypeStruct((256, 256), jnp.float32),
        compiler_params=pltpu.CompilerParams(vmem_limit_bytes=SMALL_VMEM),
    )(mine, other)


def ring_permutation(s, t):
    index = lambda ylo, core, yhi: (ylo * 2 + core) * 2 + yhi
    return [
        (index(ylo, core, yhi), index(ylo ^ t, yhi, core ^ s))
        for ylo in range(2)
        for core in range(2)
        for yhi in range(2)
    ]


def flip_permutation(s, t):
    index = lambda ylo, core, yhi: (ylo * 2 + core) * 2 + yhi
    return [
        (index(ylo, core, yhi), index(ylo ^ t, core, yhi ^ s))
        for ylo in range(2)
        for core in range(2)
        for yhi in range(2)
    ]


def ring_steps(shift):
    sign = (1, -1)
    return [(x * 2 + core, (x + sign[core] * shift) % 4 * 2 + core) for x in range(4) for core in range(2)]


def neighbour_planes():
    other = lambda z, core: ((z + core) ^ 1) - core
    return [(z * 2 + core, other(z, core) % 16 * 2 + core) for z in range(16) for core in range(2)]


def encode(terms):
    root = jnp.sqrt(jnp.abs(terms) * SCALE)
    return jnp.where(terms < 0, -root, root).astype(jnp.float16)


def decode(codes):
    root = codes.astype(jnp.float32)
    return root * jnp.abs(root) * (1.0 / SCALE)


def body(factors, occ_energies, virt_energies, freq_grid, occ_index, virt_index, freq_index):
    planes = lax.all_to_all(pack(factors), "z", split_axis=0, concat_axis=0, tiled=True)
    rows = planes.reshape(-1, planes.shape[2])

    own = lax.ppermute(rows, Y_RING, ring_permutation(0, 0))
    step, opposite, back = [lax.ppermute(own, ("x", "core"), ring_steps(shift)) for shift in (1, 2, 3)]
    q_blocks = [
        own,
        lax.ppermute(own, Y_RING, flip_permutation(0, 1)),
        lax.ppermute(rows, Y_RING, ring_permutation(1, 0)),
        lax.ppermute(own, Y_RING, flip_permutation(1, 1)),
    ]
    weight = weights(occ_index, occ_energies, freq_grid, freq_index, virt_energies, virt_index, rows)
    weight = lax.ppermute(weight, Y_RING, ring_permutation(0, 0))

    keep, send = product(weight, own, back, *q_blocks[::-1], opposite, step)
    got = lax.ppermute(send, "core", [(0, 1), (1, 0)])
    passed = lax.ppermute(encode(keep[1] + got[1]), ("z", "core"), neighbour_planes())
    pairs = encode(keep[0] + got[0] + decode(passed))
    terms = lax.all_to_all(
        pairs.reshape(256, 8, 128), ("z", "ylo", "x", "core"), split_axis=0, concat_axis=0, tiled=True
    )
    mine = jnp.sum(decode(terms).reshape(8, 2, 16, 8, 128), axis=0)
    other = lax.ppermute(mine, "yhi", [(0, 1), (1, 0)])
    return assemble(mine, other)


def solution(mesh):
    fine = Mesh(mesh.devices.reshape(16, 2, 4, 2, 2), AXES)
    columns = ("ylo", "x", "core")
    return jax.shard_map(
        body,
        mesh=fine,
        in_specs=(P("yhi", ("z",) + columns, None), P(), P(), P(), P("yhi"), P(), P()),
        out_specs=P("z", columns),
        check_vma=False,
    )
```
